128 devices in a mesh: row: 4 (over x_lo, core), col: 4 (over z), chan: 8 (over y, x_hi).
Axes of the slice: x: 4 (x_hi: 2, x_lo: 2; x = x_hi * 2 + x_lo), y: 4, z: 4, core: 2. Of those that a mesh axis runs over, the one named last changes fastest.
Arguments:
- visibilities: bfloat16 [64, 1, 4, 2, 512, 512], P('chan', None, None, None, 'row', 'col'), may hold values from -6 to 6
- model: bfloat16 [8, 64, 1, 4, 2, 512, 512], P(None, 'chan', None, None, None, 'row', 'col'), may hold values from -6 to 6
- flags: int32 [64, 512, 512], P('chan', 'row', 'col'), may hold values 0 or 1
- gains: float32 [8, 2, 2, 64, 512], P(None, None, None, 'chan'), may hold values from -3 to 3
- kernel: float32 [5], replicated, may hold values from 0.2 to 1
Outputs:
- gains_out: float32 [8, 2, 2, 64, 512], P(None, None, None, 'chan')
- residual: bfloat16 [64, 1, 4, 2, 512, 512], P('chan', None, None, None, 'row', 'col')
The draws below stay inside these ranges and needn't reach their ends.
All inputs are finite; a program needn't handle non-finite values. No bound on the sum of `flags` on one device may be relied on, other than what follows from the above.
Results may differ from the reference program's by a relative error of at most 0.001.
Values sent between devices are 32-bit elements; how exact they have to be, the bound alone decides.
No kernel may reach another device: no remote copies, remote signals or barrier semaphores. Data moves between devices by JAX's collectives and lax.ppermute only.
A program may use at most 192 MiB of HBM per device.

```python
import math
import jax
import jax.numpy as jnp
import numpy as np
from jax import lax

STATIONS = 512
DIRS = 8
TIMES = 1
ITERS = 3
HALF = 2
CHANNELS = 64


def plant(drawn, key, low, largest):
    index_at = [jax.random.randint(jax.random.fold_in(key, axis), (), 0, length) for axis, length in enumerate(drawn.shape)]
    main_axis = drawn.shape.index(max(drawn.shape))
    next_to = index_at[:main_axis] + [(index_at[main_axis] + 1) % drawn.shape[main_axis]] + index_at[main_axis + 1:]
    return drawn.at[tuple(index_at)].set(low).at[tuple(next_to)].set(largest)


def shard_levels(key, extent, cuts, low, top_value):
    def one(dim, blocks):
        heights = jax.random.uniform(jax.random.fold_in(jax.random.fold_in(key, 6), dim), (blocks,), jnp.float32, low / len(cuts), top_value / len(cuts))
        return jnp.repeat(jnp.exp(heights), extent[dim] // blocks).reshape((-1,) + (1,) * (len(extent) - dim - 1))

    factor_of = one(*cuts[0])
    for cut in cuts[1:]:
        factor_of = factor_of * one(*cut)
    return factor_of


def noise(rng, extent, deviation, most, cuts=(), held_as=jnp.bfloat16):
    entries = jax.random.normal(rng, extent, jnp.float32) * deviation
    if len(cuts) > 0:
        entries = shard_levels(rng, extent, cuts, -0.22, 0.18) * entries
    return jnp.clip(entries, min=-most, max=most).astype(held_as)


def setup_inputs(seed: int = 0) -> dict:
    streams_of = jax.random.split(jax.random.key(seed), 6)
    return {
        "visibilities": noise(streams_of[0], (CHANNELS, TIMES, 4, 2, STATIONS, STATIONS), 1.0, 6.0, ((0, 8), (4, 4), (5, 4))),
        "model": noise(streams_of[1], (DIRS, CHANNELS, TIMES, 4, 2, STATIONS, STATIONS), 1.0, 6.0, ((1, 8), (5, 4), (6, 4))),
        "flags": plant((jax.random.randint(streams_of[2], (CHANNELS, STATIONS, STATIONS), 0, 10) < 9).astype(jnp.int32), jax.random.fold_in(streams_of[2], 1), 0, 1),
        "gains": noise(streams_of[3], (DIRS, 2, 2, CHANNELS, STATIONS), 0.8, 3.0, ((3, 8),), jnp.float32),
        "kernel": jnp.clip(jnp.exp(jax.random.uniform(streams_of[4], (2 * HALF + 1,), jnp.float32, math.log(0.2), math.log(1.0))), 0.2, 1.0),
    }


A_POL = np.array([0, 0, 1, 1])
B_POL = np.array([0, 1, 0, 1])
LAMBDA = 1.0


def block_terms(vis_c, model_c, weight, gain_rows, gain_cols):
    count = gain_rows.shape[0]
    rows = gain_rows.shape[3]
    cols = gain_cols.shape[3]
    rows_re = gain_rows[:, 0][:, A_POL][:, None, :, :, None]
    rows_im = gain_rows[:, 1][:, A_POL][:, None, :, :, None]
    cols_re = gain_cols[:, 0][:, B_POL][:, None, :, None, :]
    cols_im = gain_cols[:, 1][:, B_POL][:, None, :, None, :]
    model_re = model_c[:, :, :, 0].astype(jnp.float32)
    model_im = model_c[:, :, :, 1].astype(jnp.float32)
    along_re = model_re * cols_re + model_im * cols_im
    along_im = model_im * cols_re - model_re * cols_im
    guess_re = rows_re * along_re - rows_im * along_im
    guess_im = rows_re * along_im + rows_im * along_re
    mask = weight[None, None, None]
    resid_re = vis_c[:, :, 0].astype(jnp.float32) - jnp.sum(guess_re, axis=0)
    resid_im = vis_c[:, :, 1].astype(jnp.float32) - jnp.sum(guess_im, axis=0)
    peeled_re = resid_re[None] + guess_re
    peeled_im = resid_im[None] + guess_im
    paired_re = rows_re * model_re - rows_im * model_im
    paired_im = rows_re * model_im + rows_im * model_re
    row_top_re = jnp.sum(mask * (peeled_re * along_re + peeled_im * along_im), axis=(1, 4))
    row_top_im = jnp.sum(mask * (peeled_im * along_re - peeled_re * along_im), axis=(1, 4))
    row_bottom = jnp.sum(mask * (along_re * along_re + along_im * along_im), axis=(1, 4))
    col_top_re = jnp.sum(mask * (peeled_re * paired_re + peeled_im * paired_im), axis=(1, 3))
    col_top_im = jnp.sum(mask * (peeled_re * paired_im - peeled_im * paired_re), axis=(1, 3))
    col_bottom = jnp.sum(mask * (paired_re * paired_re + paired_im * paired_im), axis=(1, 3))
    row_numer = jnp.stack([row_top_re, row_top_im], 1).reshape(count, 2, 2, 2, rows).sum(3)
    row_denom = row_bottom.reshape(count, 2, 2, rows).sum(2)
    col_numer = jnp.stack([col_top_re, col_top_im], 1).reshape(count, 2, 2, 2, cols).sum(2)
    col_denom = col_bottom.reshape(count, 2, 2, cols).sum(1)
    residual = (jnp.stack([resid_re, resid_im], 2) * weight).astype(jnp.bfloat16)
    return row_numer, row_denom, col_numer, col_denom, residual


def renew(gains_now, numer, denom):
    solved = numer / (denom[:, None] + LAMBDA)
    return 0.5 * (gains_now + solved)


def smooth(averaged, kernel):
    span = kernel.shape[0]
    reach = span // 2
    count = averaged.shape[3]
    padded = jnp.pad(averaged, ((0, 0), (0, 0), (0, 0), (reach, reach), (0, 0)))
    ones = jnp.pad(jnp.ones((count,), jnp.float32), (reach, reach))
    total = jnp.zeros(averaged.shape, jnp.float32)
    coverage = jnp.zeros((count,), jnp.float32)
    for offset in range(span):
        total = total + kernel[offset] * padded[:, :, :, offset:offset + count]
        coverage = coverage + kernel[offset] * ones[offset:offset + count]
    return total / coverage[:, None]


def reference(visibilities, model, flags, gains, kernel):
    channels = visibilities.shape[0]

    def terms(gains_now, channel):
        vis_c = lax.dynamic_index_in_dim(visibilities, channel, 0, keepdims=False)
        model_c = lax.dynamic_index_in_dim(model, channel, 1, keepdims=False)
        weight = lax.dynamic_index_in_dim(flags, channel, 0, keepdims=False).astype(jnp.float32)
        gain_c = lax.dynamic_index_in_dim(gains_now, channel, 3, keepdims=False)
        return block_terms(vis_c, model_c, weight, gain_c, gain_c)

    def sums(gains_now):
        def one(channel):
            row_numer, row_denom, col_numer, col_denom, _ = terms(gains_now, channel)
            return row_numer + col_numer, row_denom + col_denom

        numer, denom = lax.map(one, jnp.arange(channels, dtype=jnp.int32))
        return jnp.moveaxis(numer, 0, 3), jnp.moveaxis(denom, 0, 2)

    for sweep in range(ITERS):
        numer, denom = sums(gains)
        gains = smooth(renew(gains, numer, denom), kernel)

    def final(channel):
        return terms(gains, channel)[4]

    residual = lax.map(final, jnp.arange(channels, dtype=jnp.int32))
    return gains, residual
```

```python
import functools

import jax
import jax.numpy as jnp
import numpy as np
from jax import lax
from jax.experimental import pallas as pl
from jax.experimental.pallas import tpu as pltpu
from jax.sharding import PartitionSpec as P

ITERS = 3
GRID = ("row", "col")
TILE = 16


def spread_matrix(count):
    spread = np.zeros((count, 2, 2, count, 2, TILE), np.float32)
    for k in range(count):
        spread[k, 0, 0, k, 0] = 1.0
        spread[k, 1, 0, k, 1] = -1.0
        spread[k, 1, 1, k, 0] = 1.0
        spread[k, 0, 1, k, 1] = 1.0
    return spread.reshape(2 * count, 4 * count * TILE)


def split(value):
    high = value.astype(jnp.bfloat16)
    low = (value - high.astype(jnp.float32)).astype(jnp.bfloat16)
    return high, low


def kernel(first, final, place, *refs):
    refs = list(refs)
    take = refs.pop
    model, vis, flags, spread = take(0), take(0), take(0), take(0)
    row_parts = [take(0) for _ in range(1 if first else 4)]
    col_parts = [take(0) for _ in range(1 if first else 4)]
    if final:
        resid = take(0)
    else:
        row_out = [take(0) for _ in range(4)]
        col_out = [take(0) for _ in range(4)]
    g_row, g_col, g_mat, w_row, w_col, left, masked, terms = refs
    count = model.shape[0]
    channel = pl.program_id(0)
    me_row, me_col = place[0], place[1]
    f32, bf16 = jnp.float32, jnp.bfloat16

    @pl.when(channel == 0)
    def prepare():
        if first:
            g_row[...] = row_parts[0][...]
            g_col[...] = col_parts[0][...]
        else:
            for m in range(4):
                at = lax.rem(me_col + 4 - m, 4)
                g_row[pl.ds(at * 2, 2)] = row_parts[m][...]
                at = lax.rem(me_row + 4 - m, 4)
                g_col[pl.ds(at * 2, 2)] = col_parts[m][...]
        for k in range(count):
            for pol in range(2):
                lanes = slice(pol * 128, pol * 128 + 128)
                for part in range(2):
                    g_mat[:, 2 * k + part, lanes] = g_row[k, part, pol]
                if not final:
                    for source, weights in ((g_row, w_row), (g_col, w_col)):
                        re, im = source[k, 0, pol], source[k, 1, pol]
                        for n, value in enumerate((re, im, re * re + im * im)):
                            high = value.astype(bf16).astype(f32)
                            weights[:, k, n, lanes] = high
                            weights[:, k, 4 + n, lanes] = value - high
                        zero = jnp.zeros_like(re)
                        for n in (3, 7, 8, 9, 10, 11, 12, 13, 14, 15):
                            weights[:, k, n, lanes] = zero

    gains_c = jnp.transpose(g_mat[channel])
    high, low = split(gains_c)
    width = 2 * count * TILE
    same = (
        lax.broadcasted_iota(jnp.int32, (128, 2 * width), 0) % TILE
        == lax.broadcasted_iota(jnp.int32, (128, 2 * width), 1) % TILE
    )
    for h, value in enumerate((high, low)):
        for pol in range(2):
            wide = jnp.dot(value[pol * 128 : pol * 128 + 128], spread[...], preferred_element_type=f32)
            wide = jnp.where(same, wide, 0.0).astype(bf16)
            for part in range(2):
                left[pol, :, (2 * h + part) * TILE : (2 * h + part + 1) * TILE, :] = wide[
                    :, part * width : (part + 1) * width
                ].reshape(128 // TILE, TILE, width)

    def residual_tile(step, _):
        pol, tile = step // 8, step % 8
        rows = pl.ds(pl.multiple_of(tile * TILE, TILE), TILE)
        stacks = []
        for b in range(2):
            parts, lows = [], []
            for k in range(count):
                m_re = model[k, 0, 0, 2 * pol + b, 0, rows, :].astype(f32)
                m_im = model[k, 0, 0, 2 * pol + b, 1, rows, :].astype(f32)
                q_re = g_col[k, 0, b, pl.ds(channel, 1), :]
                q_im = g_col[k, 1, b, pl.ds(channel, 1), :]
                z_re = m_re * q_re + m_im * q_im
                z_im = m_im * q_re - m_re * q_im
                for z in (z_re, z_im):
                    if final:
                        z_high, z_low = split(z)
                        parts.append(z_high)
                        lows.append(z_low)
                    else:
                        parts.append(z.astype(bf16))
            stacks.append((jnp.concatenate(parts, 0), jnp.concatenate(lows, 0) if final else None))
        gains_t = left[pol, tile]
        guess = jnp.dot(gains_t, jnp.concatenate([s[0] for s in stacks], 1), preferred_element_type=f32)
        if final:
            guess += jnp.dot(gains_t, jnp.concatenate([s[1] for s in stacks], 1), preferred_element_type=f32)
        weight = flags[0, rows, :].astype(f32)
        out_rows = pl.ds(pl.multiple_of(step * TILE, TILE), TILE)
        for b in range(2):
            for part in range(2):
                lanes = slice(b * 128, b * 128 + 128)
                total = (
                    guess[part * TILE : (part + 1) * TILE, lanes]
                    + guess[(2 + part) * TILE : (3 + part) * TILE, lanes]
                )
                seen = vis[0, 0, 2 * pol + b, part, rows, :].astype(f32)
                value = (seen - total) * weight
                if final:
                    resid[0, 0, 2 * pol + b, part, rows, :] = value.astype(bf16)
                else:
                    masked[part, out_rows, lanes] = value
        return 0

    lax.fori_loop(0, 16, residual_tile, 0, unroll=4)
    if final:
        return

    def product_tile(step, _):
        pol, tile = step // 8, step % 8
        rows = pl.ds(pl.multiple_of(tile * TILE, TILE), TILE)
        weight = flags[0, rows, :].astype(f32).astype(bf16)
        out_rows = pl.ds(pl.multiple_of(step * TILE, TILE), TILE)
        for b in range(2):
            lanes = slice(b * 128, b * 128 + 128)
            r_re = masked[0, out_rows, lanes]
            r_im = masked[1, out_rows, lanes]
            for k in range(count):
                m_re = model[k, 0, 0, 2 * pol + b, 0, rows, :]
                m_im = model[k, 0, 0, 2 * pol + b, 1, rows, :]
                terms[k, 4, out_rows, lanes] = (m_re * m_re + m_im * m_im) * weight
                m_re, m_im = m_re.astype(f32), m_im.astype(f32)
                for x, value in enumerate((r_re * m_re + r_im * m_im, r_im * m_re - r_re * m_im)):
                    high, low = split(value)
                    terms[k, 2 * x, out_rows, lanes] = high
                    terms[k, 2 * x + 1, out_rows, lanes] = low
        return 0

    lax.fori_loop(0, 16, product_tile, 0, unroll=2)

    for m in range(4):
        for outs, mine, gains in ((row_out[m], me_col, g_row), (col_out[m], me_row, g_col)):
            for two in range(2):
                k = lax.rem(mine + m, 4) * 2 + two
                is_row = gains is g_row
                if is_row:
                    weights = w_col[channel, k].astype(bf16)
                    sums = [
                        lax.dot_general(weights, terms[k, x], (((1,), (1,)), ((), ())), preferred_element_type=f32)
                        for x in range(5)
                    ]
                else:
                    weights = w_row[channel, k].astype(bf16)
                    sums = [jnp.dot(weights, terms[k, x], preferred_element_type=f32) for x in range(5)]
                sums = [sums[0] + sums[1], sums[2] + sums[3], sums[4]]
                sums = [s[0:4] + s[4:8] for s in sums]
                if is_row:
                    top_re = sums[0][0:1] - sums[1][1:2]
                    top_im = sums[0][1:2] + sums[1][0:1]
                else:
                    top_re = sums[0][0:1] + sums[1][1:2]
                    top_im = sums[0][1:2] - sums[1][0:1]
                below = sums[2][2:3]
                factor = 2.0 * below + 0.25 if is_row else 2.0 * below
                for pol in range(2):
                    lanes = slice(pol * 128, pol * 128 + 128)
                    at = pl.ds(channel, 1)
                    outs[two, 0, pol, at, :] = top_re[:, lanes] + gains[k, 0, pol, at, :] * factor[:, lanes]
                    outs[two, 1, pol, at, :] = top_im[:, lanes] + gains[k, 1, pol, at, :] * factor[:, lanes]
                    outs[two, 2, pol, at, :] = below[:, lanes]


def sweep(first, final, place, model, vis, flags, row_parts, col_parts):
    count, channels = model.shape[0], model.shape[1]
    f32, bf16 = jnp.float32, jnp.bfloat16
    spread = jnp.asarray(spread_matrix(count), bf16)

    def whole(shape):
        return pl.BlockSpec(shape, lambda c, place: (0,) * len(shape))

    in_specs = [
        pl.BlockSpec((count, 1, 1, 4, 2, 128, 128), lambda c, place: (0, c, 0, 0, 0, 0, 0)),
        pl.BlockSpec((1, 1, 4, 2, 128, 128), lambda c, place: (c, 0, 0, 0, 0, 0)),
        pl.BlockSpec((1, 128, 128), lambda c, place: (c, 0, 0)),
        whole(spread.shape),
    ]
    if first:
        block = (count, 2, 2, channels, 128)
        in_specs += [
            pl.BlockSpec(block, lambda c, place: (0, 0, 0, 0, place[0])),
            pl.BlockSpec(block, lambda c, place: (0, 0, 0, 0, place[1])),
        ]
    else:
        in_specs += [whole(part.shape) for part in (*row_parts, *col_parts)]
    if final:
        out_shape = jax.ShapeDtypeStruct(vis.shape, bf16)
        out_specs = pl.BlockSpec((1, 1, 4, 2, 128, 128), lambda c, place: (c, 0, 0, 0, 0, 0))
    else:
        shape = (count // 4, 3, 2, channels, 128)
        out_shape = [jax.ShapeDtypeStruct(shape, f32)] * 8
        out_specs = [whole(shape)] * 8
    return pl.pallas_call(
        functools.partial(kernel, first, final),
        out_shape=out_shape,
        grid_spec=pltpu.PrefetchScalarGridSpec(
            num_scalar_prefetch=1,
            grid=(channels,),
            in_specs=in_specs,
            out_specs=out_specs,
            scratch_shapes=[
                pltpu.VMEM((count, 2, 2, channels, 128), f32),
                pltpu.VMEM((count, 2, 2, channels, 128), f32),
                pltpu.VMEM((channels, 2 * count, 256), f32),
                pltpu.VMEM((channels, count, 16, 256), f32),
                pltpu.VMEM((channels, count, 16, 256), f32),
                pltpu.VMEM((2, 8, 4 * TILE, 2 * count * TILE), bf16),
                pltpu.VMEM((2, 256, 256), f32),
                pltpu.VMEM((count, 5, 256, 256), bf16),
            ],
        ),
        compiler_params=pltpu.CompilerParams(vmem_limit_bytes=48 * 1024 * 1024),
        cost_estimate=pl.CostEstimate(flops=10**10, bytes_accessed=20 * 10**6, transcendentals=0),
    )(place, model, vis, flags, spread, *row_parts, *col_parts)


def move(block, target):
    pairs = []
    for row in range(4):
        for col in range(4):
            to_row, to_col = target(row, col)
            pairs.append((row * 4 + col, to_row * 4 + to_col))
    return lax.ppermute(block, GRID, pairs)


def smooth(averaged, kernel_weights, first, total_channels):
    span = kernel_weights.shape[0]
    reach = span // 2
    channels = averaged.shape[3]
    chans = lax.axis_size("chan")
    forward = [(i, i + 1) for i in range(chans - 1)]
    backward = [(i + 1, i) for i in range(chans - 1)]
    low = lax.ppermute(averaged[:, :, :, channels - reach :], "chan", forward)
    high = lax.ppermute(averaged[:, :, :, :reach], "chan", backward)
    padded = jnp.concatenate([low, averaged, high], axis=3)
    index = first + jnp.arange(channels, dtype=jnp.int32)
    total = jnp.zeros(averaged.shape, jnp.float32)
    coverage = jnp.zeros((channels,), jnp.float32)
    for offset in range(span):
        total = total + kernel_weights[offset] * padded[:, :, :, offset : offset + channels]
        source = index + offset - reach
        inside = ((source >= 0) & (source < total_channels)).astype(jnp.float32)
        coverage = coverage + kernel_weights[offset] * inside
    return total / coverage[:, None]


def in_order(parts, mine):
    chunks = []
    for chunk in range(4):
        value = parts[0]
        for m in range(1, 4):
            value = jnp.where(lax.rem(mine + 4 - m, 4) == chunk, parts[m], value)
        chunks.append(value)
    return jnp.concatenate(chunks, 0)


def local(visibilities, model, flags, gains, kernel_weights):
    channels = visibilities.shape[0]
    me_row, me_col = lax.axis_index("row"), lax.axis_index("col")
    place = jnp.stack([me_row, me_col]).astype(jnp.int32)
    first = lax.axis_index("chan") * channels
    total_channels = channels * lax.axis_size("chan")
    row_parts, col_parts = [gains], [gains]
    for step in range(ITERS):
        outs = sweep(step == 0, False, place, model, visibilities, flags, row_parts, col_parts)
        total = outs[0]
        for m in range(1, 4):
            total = total + move(outs[m], lambda i, j, m=m: (i, (j + m) % 4))
        for m in range(4):
            total = total + move(outs[4 + m], lambda i, j, m=m: (j, (i + m) % 4))
        averaged = 0.5 * total[:, :2] / (total[:, 2:] + 1.0)
        mine = smooth(averaged, kernel_weights, first, total_channels)
        row_parts = [mine] + [move(mine, lambda i, j, m=m: (i, (j + m) % 4)) for m in range(1, 4)]
        col_parts = [move(mine, lambda i, j, m=m: ((j + m) % 4, i)) for m in range(4)]
    block = in_order(row_parts, me_col)
    blocks = [block] + [move(block, lambda i, j, m=m: ((i + m) % 4, j)) for m in range(1, 4)]
    residual = sweep(False, True, place, model, visibilities, flags, row_parts, col_parts)
    columns = []
    for chunk in range(4):
        value = blocks[0]
        for m in range(1, 4):
            value = jnp.where(lax.rem(me_row + 4 - m, 4) == chunk, blocks[m], value)
        columns.append(value)
    return jnp.concatenate(columns, 4), residual


def solution(mesh):
    placed = (
        P("chan", None, None, None, "row", "col"),
        P(None, "chan", None, None, None, "row", "col"),
        P("chan", "row", "col"),
        P(None, None, None, "chan", None),
        P(),
    )
    return jax.shard_map(
        local,
        mesh=mesh,
        in_specs=placed,
        out_specs=(P(None, None, None, "chan", None), P("chan", None, None, None, "row", "col")),
        check_vma=False,
    )
```

```python
import functools

import jax
import jax.numpy as jnp
import numpy as np
from jax import lax
from jax.experimental import pallas as pl
from jax.experimental.pallas import tpu as pltpu
from jax.sharding import PartitionSpec as P

ITERS = 3
GRID = ("row", "col")
VMEM_LIMIT = 60 * 1024 * 1024
TILE = 16


def spread_matrix(count):
    spread = np.zeros((count, 2, 2, count, 2, TILE), np.float32)
    for k in range(count):
        spread[k, 0, 0, k, 0] = 1.0
        spread[k, 1, 0, k, 1] = -1.0
        spread[k, 1, 1, k, 0] = 1.0
        spread[k, 0, 1, k, 1] = 1.0
    return spread.reshape(2 * count, 4 * count * TILE)


def split(value):
    high = value.astype(jnp.bfloat16)
    low = (value - high.astype(jnp.float32)).astype(jnp.bfloat16)
    return high, low


def kernel(first, precise, final, place, *refs):
    refs = list(refs)
    take = refs.pop
    model, vis, flags, spread = take(0), take(0), take(0), take(0)
    if first:
        row_in, col_in = take(0), take(0)
    else:
        gains_in = take(0)
    if final:
        resid, gains_out = take(0), take(0)
    else:
        sums_out = take(0)
    g_row, g_col, g_mat, w_row, w_col, left, masked, raw = refs
    count = model.shape[0]
    channel = pl.program_id(0)
    me_row, me_col = place[0], place[1]
    f32, bf16 = jnp.float32, jnp.bfloat16

    @pl.when(channel == 0)
    def prepare():
        if first:
            g_row[...] = row_in[...]
            g_col[...] = col_in[...]
        else:
            for k in range(count):
                for pol in range(2):
                    for part in range(2):
                        if final:
                            g_row[k, part, pol] = gains_in[2 * k + pol, me_row, part]
                            g_col[k, part, pol] = gains_in[2 * k + pol, me_col, part]
                            for block in range(4):
                                lanes = slice(block * 128, block * 128 + 128)
                                gains_out[k, part, pol, :, lanes] = gains_in[2 * k + pol, block, part]
                        else:
                            g_row[k, part, pol] = gains_in[2 * k + pol, 0, part]
                            g_col[k, part, pol] = gains_in[2 * k + pol, 1, part]
        for k in range(count):
            for pol in range(2):
                lanes = slice(pol * 128, pol * 128 + 128)
                for part in range(2):
                    g_mat[:, 2 * k + part, lanes] = g_row[k, part, pol]
                if not final:
                    for source, weights in ((g_row, w_row), (g_col, w_col)):
                        re, im = source[k, 0, pol], source[k, 1, pol]
                        for n, value in enumerate((re, im, re * re + im * im)):
                            high = value.astype(bf16).astype(f32)
                            weights[:, k, n, lanes] = high
                            weights[:, k, 4 + n, lanes] = value - high
                        zero = jnp.zeros_like(re)
                        for n in (3, 7, 8, 9, 10, 11, 12, 13, 14, 15):
                            weights[:, k, n, lanes] = zero

    gains_c = jnp.transpose(g_mat[channel])
    high, low = split(gains_c)
    width = 2 * count * TILE
    same = (
        lax.broadcasted_iota(jnp.int32, (128, 2 * width), 0) % TILE
        == lax.broadcasted_iota(jnp.int32, (128, 2 * width), 1) % TILE
    )
    for h, value in enumerate((high, low)):
        for pol in range(2):
            wide = jnp.dot(value[pol * 128 : pol * 128 + 128], spread[...], preferred_element_type=f32)
            wide = jnp.where(same, wide, 0.0).astype(bf16)
            for part in range(2):
                left[pol, :, (2 * h + part) * TILE : (2 * h + part + 1) * TILE, :] = wide[
                    :, part * width : (part + 1) * width
                ].reshape(128 // TILE, TILE, width)

    def residual_tile(step, _):
        pol, tile = step // 8, step % 8
        rows = pl.ds(pl.multiple_of(tile * TILE, TILE), TILE)
        stacks = []
        for b in range(2):
            parts, lows = [], []
            for k in range(count):
                m_re = model[k, 0, 0, 2 * pol + b, 0, rows, :].astype(f32)
                m_im = model[k, 0, 0, 2 * pol + b, 1, rows, :].astype(f32)
                q_re = g_col[k, 0, b, pl.ds(channel, 1), :]
                q_im = g_col[k, 1, b, pl.ds(channel, 1), :]
                z_re = m_re * q_re + m_im * q_im
                z_im = m_im * q_re - m_re * q_im
                for z in (z_re, z_im):
                    if final:
                        z_high, z_low = split(z)
                        parts.append(z_high)
                        lows.append(z_low)
                    else:
                        parts.append(z.astype(bf16))
            stacks.append((jnp.concatenate(parts, 0), jnp.concatenate(lows, 0) if final else None))
        gains_t = left[pol, tile]
        guess = jnp.dot(gains_t, jnp.concatenate([s[0] for s in stacks], 1), preferred_element_type=f32)
        if final:
            guess += jnp.dot(gains_t, jnp.concatenate([s[1] for s in stacks], 1), preferred_element_type=f32)
        weight = flags[0, rows, :].astype(f32)
        out_rows = pl.ds(pl.multiple_of(step * TILE, TILE), TILE)
        for b in range(2):
            for part in range(2):
                lanes = slice(b * 128, b * 128 + 128)
                total = (
                    guess[part * TILE : (part + 1) * TILE, lanes]
                    + guess[(2 + part) * TILE : (3 + part) * TILE, lanes]
                )
                seen = vis[0, 0, 2 * pol + b, part, rows, :].astype(f32)
                value = (seen - total) * weight
                if final:
                    resid[0, 0, 2 * pol + b, part, rows, :] = value.astype(bf16)
                else:
                    masked[part, out_rows, lanes] = value
        return 0

    if final:
        lax.fori_loop(0, 16, residual_tile, 0, unroll=4)
        return

    lax.fori_loop(0, 16, residual_tile, 0, unroll=4)
    weight = flags[0].astype(f32).astype(bf16)

    def sums(k, _):
        kinds = 5 if precise else 3
        planes = [[] for _ in range(kinds)]
        for pol in range(2):
            halves = [[] for _ in range(kinds)]
            for b in range(2):
                low_re = model[k, 0, 0, 2 * pol + b, 0]
                low_im = model[k, 0, 0, 2 * pol + b, 1]
                r_re = masked[0, pol * 128 : pol * 128 + 128, b * 128 : b * 128 + 128]
                r_im = masked[1, pol * 128 : pol * 128 + 128, b * 128 : b * 128 + 128]
                m_re, m_im = low_re.astype(f32), low_im.astype(f32)
                values = (r_re * m_re + r_im * m_im, r_im * m_re - r_re * m_im)
                values = split(values[0]) + split(values[1]) if precise else tuple(v.astype(bf16) for v in values)
                values += ((low_re * low_re + low_im * low_im) * weight,)
                for half, value in zip(halves, values):
                    half.append(value)
            for plane, half in zip(planes, halves):
                plane.append(jnp.concatenate(half, 1))
        planes = [jnp.concatenate(plane, 0) for plane in planes]
        by_q, by_p = w_col[channel, k].astype(bf16), w_row[channel, k].astype(bf16)
        over_q = [
            lax.dot_general(by_q, plane, (((1,), (1,)), ((), ())), preferred_element_type=f32) for plane in planes
        ]
        over_p = [jnp.dot(by_p, plane, preferred_element_type=f32) for plane in planes]
        for side, found in enumerate((over_q, over_p)):
            if precise:
                found = (found[0] + found[1], found[2] + found[3], found[4])
            for x, value in enumerate(found):
                raw[side, channel, k, x] = value[0:4] + value[4:8]
        return 0

    lax.fori_loop(0, count, sums, 0)
    last = pl.num_programs(0) - 1

    @pl.when(channel == last)
    def finish():
        for side, gains in ((0, g_row), (1, g_col)):
            sign = 1.0 if side == 0 else -1.0
            for k in range(count):
                for pol in range(2):
                    lanes = slice(pol * 128, pol * 128 + 128)
                    take_row = lambda x, n: raw[side, :, k, x, n, lanes]
                    denom = take_row(2, 2)
                    factor = 2.0 * denom + 0.25 if side == 0 else 2.0 * denom
                    top_re = take_row(0, 0) - sign * take_row(1, 1)
                    top_im = take_row(0, 1) + sign * take_row(1, 0)
                    sums_out[2 * k + pol, side, 0] = top_re + gains[k, 0, pol] * factor
                    sums_out[2 * k + pol, side, 1] = top_im + gains[k, 1, pol] * factor
                    sums_out[2 * k + pol, side, 2] = denom


def final_kernel(place, model, vis, flags, gains_in, resid, gains_out, p_rows, p_cols, q_rows):
    count = model.shape[0]
    channel = pl.program_id(0)
    me_row, me_col = place[0], place[1]
    f32, bf16 = jnp.float32, jnp.bfloat16

    @pl.when(channel == 0)
    def prepare():
        p_rows[...] = jnp.zeros_like(p_rows)
        for k in range(count):
            for pol in range(2):
                for part in range(2):
                    for block in range(4):
                        lanes = slice(block * 128, block * 128 + 128)
                        gains_out[k, part, pol, :, lanes] = gains_in[2 * k + pol, block, part]
                    p_rows[:, 2 * k + part, pol * 128 : pol * 128 + 128] = gains_in[2 * k + pol, me_row, part]
                re, im = gains_in[2 * k + pol, me_col, 0], gains_in[2 * k + pol, me_col, 1]
                for n, value in enumerate((im, re - im, re + im)):
                    q_rows[k, n, pol] = value

    p_cols[...] = jnp.transpose(p_rows[channel])

    def tile_work(step, _):
        pol, tile = step // 8, step % 8
        rows = pl.ds(pl.multiple_of(tile * TILE, TILE), TILE)
        p_tile = p_cols[pl.ds(pl.multiple_of(step * TILE, TILE), TILE), :]
        totals = [[0.0, 0.0] for _ in range(2)]
        for k in range(count):
            p_re, p_im = [jnp.broadcast_to(p_tile[:, 2 * k + n : 2 * k + n + 1], (TILE, 128)) for n in range(2)]
            for b in range(2):
                q = [q_rows[k, n, b, pl.ds(channel, 1), :] for n in range(3)]
                m_re = model[k, 0, 0, 2 * pol + b, 0, rows, :].astype(f32)
                m_im = model[k, 0, 0, 2 * pol + b, 1, rows, :].astype(f32)
                shared = q[0] * (m_re - m_im)
                z_re = m_re * q[2] - shared
                z_im = m_im * q[1] - shared
                totals[b][0] += p_re * z_re - p_im * z_im
                totals[b][1] += p_re * z_im + p_im * z_re
        weight = flags[0, rows, :].astype(f32)
        for b in range(2):
            for part in range(2):
                seen = vis[0, 0, 2 * pol + b, part, rows, :].astype(f32)
                resid[0, 0, 2 * pol + b, part, rows, :] = ((seen - totals[b][part]) * weight).astype(bf16)
        return 0

    lax.fori_loop(0, 16, tile_work, 0, unroll=2)


def finish(place, model, vis, flags, gains):
    count, channels = model.shape[0], model.shape[1]
    f32 = jnp.float32

    def whole(shape):
        return pl.BlockSpec(shape, lambda c, place: (0,) * len(shape))

    out_gains = (count, 2, 2, channels, 512)
    seen = pl.BlockSpec((1, 1, 4, 2, 128, 128), lambda c, place: (c, 0, 0, 0, 0, 0))
    return pl.pallas_call(
        final_kernel,
        out_shape=[jax.ShapeDtypeStruct(vis.shape, vis.dtype), jax.ShapeDtypeStruct(out_gains, f32)],
        grid_spec=pltpu.PrefetchScalarGridSpec(
            num_scalar_prefetch=1,
            grid=(channels,),
            in_specs=[
                pl.BlockSpec((count, 1, 1, 4, 2, 128, 128), lambda c, place: (0, c, 0, 0, 0, 0, 0)),
                seen,
                pl.BlockSpec((1, 128, 128), lambda c, place: (c, 0, 0)),
                whole(gains.shape),
            ],
            out_specs=[seen, whole(out_gains)],
            scratch_shapes=[
                pltpu.VMEM((channels, 128, 256), f32),
                pltpu.VMEM((256, 128), f32),
                pltpu.VMEM((count, 3, 2, channels, 128), f32),
            ],
        ),
        compiler_params=pltpu.CompilerParams(vmem_limit_bytes=VMEM_LIMIT),
        cost_estimate=pl.CostEstimate(flops=10**9, bytes_accessed=20 * 10**6, transcendentals=0),
    )(place, model, vis, flags, gains)


def sweep(first, precise, final, place, model, vis, flags, gains):
    count, channels = model.shape[0], model.shape[1]
    f32, bf16 = jnp.float32, jnp.bfloat16
    spread = jnp.asarray(spread_matrix(count), bf16)

    def whole(shape):
        return pl.BlockSpec(shape, lambda c, place: (0,) * len(shape))

    in_specs = [
        pl.BlockSpec((count, 1, 1, 4, 2, 128, 128), lambda c, place: (0, c, 0, 0, 0, 0, 0)),
        pl.BlockSpec((1, 1, 4, 2, 128, 128), lambda c, place: (c, 0, 0, 0, 0, 0)),
        pl.BlockSpec((1, 128, 128), lambda c, place: (c, 0, 0)),
        whole(spread.shape),
    ]
    if first:
        block = (count, 2, 2, channels, 128)
        in_specs += [
            pl.BlockSpec(block, lambda c, place: (0, 0, 0, 0, place[0])),
            pl.BlockSpec(block, lambda c, place: (0, 0, 0, 0, place[1])),
        ]
    else:
        in_specs += [whole(gains.shape)]
    if final:
        out_gains = (count, 2, 2, channels, 512)
        out_shape = [jax.ShapeDtypeStruct(vis.shape, bf16), jax.ShapeDtypeStruct(out_gains, f32)]
        out_specs = [pl.BlockSpec((1, 1, 4, 2, 128, 128), lambda c, place: (c, 0, 0, 0, 0, 0)), whole(out_gains)]
    else:
        shape = (2 * count, 2, 3, channels, 128)
        out_shape = jax.ShapeDtypeStruct(shape, f32)
        out_specs = whole(shape)
    return pl.pallas_call(
        functools.partial(kernel, first, precise, final),
        out_shape=out_shape,
        grid_spec=pltpu.PrefetchScalarGridSpec(
            num_scalar_prefetch=1,
            grid=(channels,),
            in_specs=in_specs,
            out_specs=out_specs,
            scratch_shapes=[
                pltpu.VMEM((count, 2, 2, channels, 128), f32),
                pltpu.VMEM((count, 2, 2, channels, 128), f32),
                pltpu.VMEM((channels, 2 * count, 256), f32),
                pltpu.VMEM((channels, count, 16, 256), f32),
                pltpu.VMEM((channels, count, 16, 256), f32),
                pltpu.VMEM((2, 8, 4 * TILE, 2 * count * TILE), bf16),
                pltpu.VMEM((2, 256, 256), f32),
                pltpu.VMEM((2, channels, count, 3, 4, 256), f32),
            ],
        ),
        compiler_params=pltpu.CompilerParams(vmem_limit_bytes=VMEM_LIMIT),
        cost_estimate=pl.CostEstimate(flops=10**10, bytes_accessed=20 * 10**6, transcendentals=0),
    )(place, model, vis, flags, spread, *((gains, gains) if first else (gains,)))


def smooth_kernel(everything, chan, weights, averaged, low, high, out):
    channels = averaged.shape[2]
    span = weights.shape[0]
    reach = span // 2
    index = chan[0] + lax.broadcasted_iota(jnp.int32, (channels, 128), 0)
    coverage = jnp.zeros((channels, 128), jnp.float32)
    for offset in range(span):
        source = index + (offset - reach)
        inside = ((source >= 0) & (source < chan[1])).astype(jnp.float32)
        coverage = coverage + weights[offset] * inside
    for block in range(4):
        for part in range(2):
            padded = jnp.concatenate([low[block, part], averaged[block, part], high[block, part]], 0)
            total = weights[0] * padded[0:channels]
            for offset in range(1, span):
                total = total + weights[offset] * padded[offset : offset + channels]
            value = total / coverage
            for target in range(16):
                if everything:
                    out[target, block, part] = value
                else:
                    if target // 4 == block:
                        out[target, 0, part] = value
                    if target % 4 == block:
                        out[target, 1, part] = value


def smooth(everything, averaged, kernel_weights, first, total_channels):
    reach = kernel_weights.shape[0] // 2
    channels = averaged.shape[2]
    chans = lax.axis_size("chan")
    low = lax.ppermute(averaged[:, :, channels - reach :], "chan", [(i, i + 1) for i in range(chans - 1)])
    high = lax.ppermute(averaged[:, :, :reach], "chan", [(i + 1, i) for i in range(chans - 1)])
    chan = jnp.stack([first, jnp.int32(total_channels)]).astype(jnp.int32)
    scalars = pl.BlockSpec(memory_space=pltpu.SMEM)
    blocks = pl.BlockSpec(memory_space=pltpu.VMEM)
    return pl.pallas_call(
        functools.partial(smooth_kernel, everything),
        out_shape=jax.ShapeDtypeStruct((16, 4 if everything else 2, *averaged.shape[1:]), jnp.float32),
        in_specs=[scalars, scalars, blocks, blocks, blocks],
        out_specs=blocks,
    )(chan, kernel_weights, averaged, low, high)


def local(visibilities, model, flags, gains, kernel_weights):
    channels = visibilities.shape[0]
    place = jnp.stack([lax.axis_index("row"), lax.axis_index("col")]).astype(jnp.int32)
    first = lax.axis_index("chan") * channels
    total_channels = channels * lax.axis_size("chan")
    for step in range(ITERS):
        sums = sweep(step == 0, step == ITERS - 1, False, place, model, visibilities, flags, gains)
        parts = lax.all_to_all(sums, GRID, 0, 0)
        parts = parts.reshape(4, 4, *parts.shape[1:])
        total = parts[:, :, 0].sum(1) + parts[:, :, 1].sum(0)
        averaged = 0.5 * total[:, :2] / (total[:, 2:] + 1.0)
        mine = smooth(step == ITERS - 1, averaged, kernel_weights, first, total_channels)
        gains = lax.all_to_all(mine, GRID, 0, 0)
    residual, gains_out = finish(place, model, visibilities, flags, gains)
    return gains_out, residual


def solution(mesh):
    placed = (
        P("chan", None, None, None, "row", "col"),
        P(None, "chan", None, None, None, "row", "col"),
        P("chan", "row", "col"),
        P(None, None, None, "chan", None),
        P(),
    )
    return jax.shard_map(
        local,
        mesh=mesh,
        in_specs=placed,
        out_specs=(P(None, None, None, "chan", None), P("chan", None, None, None, "row", "col")),
        check_vma=False,
    )
```

```python
import functools

import jax
import jax.numpy as jnp
import numpy as np
from jax import lax
from jax.experimental import pallas as pl
from jax.experimental.pallas import tpu as pltpu
from jax.sharding import PartitionSpec as P

ITERS = 3
GRID = ("row", "col")
VMEM_LIMIT = 60 * 1024 * 1024
TILE = 16


def spread_matrix(count):
    spread = np.zeros((count, 2, 2, count, 2, TILE), np.float32)
    for k in range(count):
        spread[k, 0, 0, k, 0] = 1.0
        spread[k, 1, 0, k, 1] = -1.0
        spread[k, 1, 1, k, 0] = 1.0
        spread[k, 0, 1, k, 1] = 1.0
    return spread.reshape(2 * count, 4 * count * TILE)


def split(value):
    high = value.astype(jnp.bfloat16)
    low = (value - high.astype(jnp.float32)).astype(jnp.bfloat16)
    return high, low


def kernel(first, precise, final, place, *refs):
    refs = list(refs)
    take = refs.pop
    model, vis, flags, spread = take(0), take(0), take(0), take(0)
    if first:
        row_in, col_in = take(0), take(0)
    else:
        gains_in = take(0)
    if final:
        resid, gains_out = take(0), take(0)
    else:
        sums_out = take(0)
    g_row, g_col, g_mat, w_row, w_col, left, masked, raw = refs
    count = model.shape[0]
    channel = pl.program_id(0)
    me_row, me_col = place[0], place[1]
    f32, bf16 = jnp.float32, jnp.bfloat16

    @pl.when(channel == 0)
    def prepare():
        if first:
            g_row[...] = row_in[...]
            g_col[...] = col_in[...]
        else:
            for k in range(count):
                for pol in range(2):
                    for part in range(2):
                        if final:
                            g_row[k, part, pol] = gains_in[2 * k + pol, me_row, part]
                            g_col[k, part, pol] = gains_in[2 * k + pol, me_col, part]
                            for block in range(4):
                                lanes = slice(block * 128, block * 128 + 128)
                                gains_out[k, part, pol, :, lanes] = gains_in[2 * k + pol, block, part]
                        else:
                            g_row[k, part, pol] = gains_in[2 * k + pol, 0, part]
                            g_col[k, part, pol] = gains_in[2 * k + pol, 1, part]
        if not final:
            w_row[...] = jnp.zeros_like(w_row)
            w_col[...] = jnp.zeros_like(w_col)
        for k in range(count):
            for pol in range(2):
                lanes = slice(pol * 128, pol * 128 + 128)
                for part in range(2):
                    g_mat[:, 2 * k + part, lanes] = g_row[k, part, pol]
                if not final:
                    for source, weights in ((g_row, w_row), (g_col, w_col)):
                        re, im = source[k, 0, pol], source[k, 1, pol]
                        for n, value in enumerate((re, im, re * re + im * im)):
                            high = value.astype(bf16).astype(f32)
                            weights[:, k, n, lanes] = high
                            weights[:, k, 4 + n, lanes] = value - high

    gains_c = jnp.transpose(g_mat[channel])
    high, low = split(gains_c)
    width = 2 * count * TILE
    same = (
        lax.broadcasted_iota(jnp.int32, (128, 2 * width), 0) % TILE
        == lax.broadcasted_iota(jnp.int32, (128, 2 * width), 1) % TILE
    )
    for h, value in enumerate((high, low)):
        for pol in range(2):
            wide = jnp.dot(value[pol * 128 : pol * 128 + 128], spread[...], preferred_element_type=f32)
            wide = jnp.where(same, wide, 0.0).astype(bf16)
            for part in range(2):
                left[pol, :, (2 * h + part) * TILE : (2 * h + part + 1) * TILE, :] = wide[
                    :, part * width : (part + 1) * width
                ].reshape(128 // TILE, TILE, width)

    def residual_tile(step, _):
        pol, tile = step // 8, step % 8
        rows = pl.ds(pl.multiple_of(tile * TILE, TILE), TILE)
        stacks = []
        for b in range(2):
            parts, lows = [], []
            for k in range(count):
                m_re = model[k, 0, 0, 2 * pol + b, 0, rows, :].astype(f32)
                m_im = model[k, 0, 0, 2 * pol + b, 1, rows, :].astype(f32)
                q_re = g_col[k, 0, b, pl.ds(channel, 1), :]
                q_im = g_col[k, 1, b, pl.ds(channel, 1), :]
                z_re = m_re * q_re + m_im * q_im
                z_im = m_im * q_re - m_re * q_im
                for z in (z_re, z_im):
                    if final:
                        z_high, z_low = split(z)
                        parts.append(z_high)
                        lows.append(z_low)
                    else:
                        parts.append(z.astype(bf16))
            stacks.append((jnp.concatenate(parts, 0), jnp.concatenate(lows, 0) if final else None))
        gains_t = left[pol, tile]
        guess = jnp.dot(gains_t, jnp.concatenate([s[0] for s in stacks], 1), preferred_element_type=f32)
        if final:
            guess += jnp.dot(gains_t, jnp.concatenate([s[1] for s in stacks], 1), preferred_element_type=f32)
        weight = flags[0, rows, :].astype(f32)
        out_rows = pl.ds(pl.multiple_of(step * TILE, TILE), TILE)
        for b in range(2):
            for part in range(2):
                lanes = slice(b * 128, b * 128 + 128)
                total = (
                    guess[part * TILE : (part + 1) * TILE, lanes]
                    + guess[(2 + part) * TILE : (3 + part) * TILE, lanes]
                )
                seen = vis[0, 0, 2 * pol + b, part, rows, :].astype(f32)
                value = (seen - total) * weight
                if final:
                    resid[0, 0, 2 * pol + b, part, rows, :] = value.astype(bf16)
                else:
                    masked[part, out_rows, lanes] = value
        return 0

    if final:
        lax.fori_loop(0, 16, residual_tile, 0, unroll=4)
        return

    lax.fori_loop(0, 16, residual_tile, 0, unroll=4)
    weight = flags[0].astype(f32).astype(bf16)

    def sums(k, _):
        kinds = 5 if precise else 3
        planes = [[] for _ in range(kinds)]
        for pol in range(2):
            halves = [[] for _ in range(kinds)]
            for b in range(2):
                low_re = model[k, 0, 0, 2 * pol + b, 0]
                low_im = model[k, 0, 0, 2 * pol + b, 1]
                r_re = masked[0, pol * 128 : pol * 128 + 128, b * 128 : b * 128 + 128]
                r_im = masked[1, pol * 128 : pol * 128 + 128, b * 128 : b * 128 + 128]
                m_re, m_im = low_re.astype(f32), low_im.astype(f32)
                values = (r_re * m_re + r_im * m_im, r_im * m_re - r_re * m_im)
                values = split(values[0]) + split(values[1]) if precise else tuple(v.astype(bf16) for v in values)
                values += ((low_re * low_re + low_im * low_im) * weight,)
                for half, value in zip(halves, values):
                    half.append(value)
            for plane, half in zip(planes, halves):
                plane.append(jnp.concatenate(half, 1))
        planes = [jnp.concatenate(plane, 0) for plane in planes]
        by_q, by_p = w_col[channel, k].astype(bf16), w_row[channel, k].astype(bf16)
        over_q = [
            lax.dot_general(by_q, plane, (((1,), (1,)), ((), ())), preferred_element_type=f32) for plane in planes
        ]
        over_p = [jnp.dot(by_p, plane, preferred_element_type=f32) for plane in planes]
        for side, found in enumerate((over_q, over_p)):
            if precise:
                found = (found[0] + found[1], found[2] + found[3], found[4])
            for x, value in enumerate(found):
                raw[side, channel, k, x] = value[0:4] + value[4:8]
        return 0

    lax.fori_loop(0, count, sums, 0, unroll=4)
    last = pl.num_programs(0) - 1

    @pl.when(channel == last)
    def finish():
        for side, gains in ((0, g_row), (1, g_col)):
            sign = 1.0 if side == 0 else -1.0
            for k in range(count):
                for pol in range(2):
                    lanes = slice(pol * 128, pol * 128 + 128)
                    take_row = lambda x, n: raw[side, :, k, x, n, lanes]
                    denom = take_row(2, 2)
                    factor = 2.0 * denom + 0.25 if side == 0 else 2.0 * denom
                    top_re = take_row(0, 0) - sign * take_row(1, 1)
                    top_im = take_row(0, 1) + sign * take_row(1, 0)
                    sums_out[2 * k + pol, side, 0] = top_re + gains[k, 0, pol] * factor
                    sums_out[2 * k + pol, side, 1] = top_im + gains[k, 1, pol] * factor
                    sums_out[2 * k + pol, side, 2] = denom


def final_kernel(place, model, vis, flags, gains_in, resid, gains_out, p_rows, p_cols, q_rows):
    count = model.shape[0]
    channel = pl.program_id(0)
    me_row, me_col = place[0], place[1]
    f32, bf16 = jnp.float32, jnp.bfloat16

    @pl.when(channel == 0)
    def prepare():
        p_rows[...] = jnp.zeros_like(p_rows)
        for k in range(count):
            for pol in range(2):
                for part in range(2):
                    for block in range(4):
                        lanes = slice(block * 128, block * 128 + 128)
                        gains_out[k, part, pol, :, lanes] = gains_in[2 * k + pol, block, part]
                    p_rows[:, 2 * k + part, pol * 128 : pol * 128 + 128] = gains_in[2 * k + pol, me_row, part]
                re, im = gains_in[2 * k + pol, me_col, 0], gains_in[2 * k + pol, me_col, 1]
                for n, value in enumerate((im, re - im, re + im)):
                    q_rows[k, n, pol] = value

    p_cols[...] = jnp.transpose(p_rows[channel])

    def tile_work(step, _):
        pol, tile = step // 8, step % 8
        rows = pl.ds(pl.multiple_of(tile * TILE, TILE), TILE)
        p_tile = p_cols[pl.ds(pl.multiple_of(step * TILE, TILE), TILE), :]
        totals = [[0.0, 0.0] for _ in range(2)]
        for k in range(count):
            p_re, p_im = [jnp.broadcast_to(p_tile[:, 2 * k + n : 2 * k + n + 1], (TILE, 128)) for n in range(2)]
            for b in range(2):
                q = [q_rows[k, n, b, pl.ds(channel, 1), :] for n in range(3)]
                m_re = model[k, 0, 0, 2 * pol + b, 0, rows, :].astype(f32)
                m_im = model[k, 0, 0, 2 * pol + b, 1, rows, :].astype(f32)
                shared = q[0] * (m_re - m_im)
                z_re = m_re * q[2] - shared
                z_im = m_im * q[1] - shared
                totals[b][0] += p_re * z_re - p_im * z_im
                totals[b][1] += p_re * z_im + p_im * z_re
        weight = flags[0, rows, :].astype(f32)
        for b in range(2):
            for part in range(2):
                seen = vis[0, 0, 2 * pol + b, part, rows, :].astype(f32)
                resid[0, 0, 2 * pol + b, part, rows, :] = ((seen - totals[b][part]) * weight).astype(bf16)
        return 0

    lax.fori_loop(0, 16, tile_work, 0, unroll=2)


def finish(place, model, vis, flags, gains):
    count, channels = model.shape[0], model.shape[1]
    f32 = jnp.float32

    def whole(shape):
        return pl.BlockSpec(shape, lambda c, place: (0,) * len(shape))

    out_gains = (count, 2, 2, channels, 512)
    seen = pl.BlockSpec((1, 1, 4, 2, 128, 128), lambda c, place: (c, 0, 0, 0, 0, 0))
    return pl.pallas_call(
        final_kernel,
        out_shape=[jax.ShapeDtypeStruct(vis.shape, vis.dtype), jax.ShapeDtypeStruct(out_gains, f32)],
        grid_spec=pltpu.PrefetchScalarGridSpec(
            num_scalar_prefetch=1,
            grid=(channels,),
            in_specs=[
                pl.BlockSpec((count, 1, 1, 4, 2, 128, 128), lambda c, place: (0, c, 0, 0, 0, 0, 0)),
                seen,
                pl.BlockSpec((1, 128, 128), lambda c, place: (c, 0, 0)),
                whole(gains.shape),
            ],
            out_specs=[seen, whole(out_gains)],
            scratch_shapes=[
                pltpu.VMEM((channels, 128, 256), f32),
                pltpu.VMEM((256, 128), f32),
                pltpu.VMEM((count, 3, 2, channels, 128), f32),
            ],
        ),
        compiler_params=pltpu.CompilerParams(vmem_limit_bytes=VMEM_LIMIT),
        cost_estimate=pl.CostEstimate(flops=10**9, bytes_accessed=20 * 10**6, transcendentals=0),
    )(place, model, vis, flags, gains)


def sweep(first, precise, final, place, model, vis, flags, gains):
    count, channels = model.shape[0], model.shape[1]
    f32, bf16 = jnp.float32, jnp.bfloat16
    spread = jnp.asarray(spread_matrix(count), bf16)

    def whole(shape):
        return pl.BlockSpec(shape, lambda c, place: (0,) * len(shape))

    in_specs = [
        pl.BlockSpec((count, 1, 1, 4, 2, 128, 128), lambda c, place: (0, c, 0, 0, 0, 0, 0)),
        pl.BlockSpec((1, 1, 4, 2, 128, 128), lambda c, place: (c, 0, 0, 0, 0, 0)),
        pl.BlockSpec((1, 128, 128), lambda c, place: (c, 0, 0)),
        whole(spread.shape),
    ]
    if first:
        block = (count, 2, 2, channels, 128)
        in_specs += [
            pl.BlockSpec(block, lambda c, place: (0, 0, 0, 0, place[0])),
            pl.BlockSpec(block, lambda c, place: (0, 0, 0, 0, place[1])),
        ]
    else:
        in_specs += [whole(gains.shape)]
    if final:
        out_gains = (count, 2, 2, channels, 512)
        out_shape = [jax.ShapeDtypeStruct(vis.shape, bf16), jax.ShapeDtypeStruct(out_gains, f32)]
        out_specs = [pl.BlockSpec((1, 1, 4, 2, 128, 128), lambda c, place: (c, 0, 0, 0, 0, 0)), whole(out_gains)]
    else:
        shape = (2 * count, 2, 3, channels, 128)
        out_shape = jax.ShapeDtypeStruct(shape, f32)
        out_specs = whole(shape)
    return pl.pallas_call(
        functools.partial(kernel, first, precise, final),
        out_shape=out_shape,
        grid_spec=pltpu.PrefetchScalarGridSpec(
            num_scalar_prefetch=1,
            grid=(channels,),
            in_specs=in_specs,
            out_specs=out_specs,
            scratch_shapes=[
                pltpu.VMEM((count, 2, 2, channels, 128), f32),
                pltpu.VMEM((count, 2, 2, channels, 128), f32),
                pltpu.VMEM((channels, 2 * count, 256), f32),
                pltpu.VMEM((channels, count, 16, 256), f32),
                pltpu.VMEM((channels, count, 16, 256), f32),
                pltpu.VMEM((2, 8, 4 * TILE, 2 * count * TILE), bf16),
                pltpu.VMEM((2, 256, 256), f32),
                pltpu.VMEM((2, channels, count, 3, 4, 256), f32),
            ],
        ),
        compiler_params=pltpu.CompilerParams(vmem_limit_bytes=VMEM_LIMIT),
        cost_estimate=pl.CostEstimate(flops=10**10, bytes_accessed=20 * 10**6, transcendentals=0),
    )(place, model, vis, flags, spread, *((gains, gains) if first else (gains,)))


def smooth_kernel(everything, chan, weights, averaged, low, high, out):
    channels = averaged.shape[2]
    span = weights.shape[0]
    reach = span // 2
    index = chan[0] + lax.broadcasted_iota(jnp.int32, (channels, 128), 0)
    coverage = jnp.zeros((channels, 128), jnp.float32)
    for offset in range(span):
        source = index + (offset - reach)
        inside = ((source >= 0) & (source < chan[1])).astype(jnp.float32)
        coverage = coverage + weights[offset] * inside
    for block in range(4):
        for part in range(2):
            padded = jnp.concatenate([low[block, part], averaged[block, part], high[block, part]], 0)
            total = weights[0] * padded[0:channels]
            for offset in range(1, span):
                total = total + weights[offset] * padded[offset : offset + channels]
            value = total / coverage
            for target in range(16):
                if everything:
                    out[target, block, part] = value
                else:
                    if target // 4 == block:
                        out[target, 0, part] = value
                    if target % 4 == block:
                        out[target, 1, part] = value


def smooth(everything, averaged, kernel_weights, first, total_channels):
    reach = kernel_weights.shape[0] // 2
    channels = averaged.shape[2]
    chans = lax.axis_size("chan")
    low = lax.ppermute(averaged[:, :, channels - reach :], "chan", [(i, i + 1) for i in range(chans - 1)])
    high = lax.ppermute(averaged[:, :, :reach], "chan", [(i + 1, i) for i in range(chans - 1)])
    chan = jnp.stack([first, jnp.int32(total_channels)]).astype(jnp.int32)
    scalars = pl.BlockSpec(memory_space=pltpu.SMEM)
    blocks = pl.BlockSpec(memory_space=pltpu.VMEM)
    return pl.pallas_call(
        functools.partial(smooth_kernel, everything),
        out_shape=jax.ShapeDtypeStruct((16, 4 if everything else 2, *averaged.shape[1:]), jnp.float32),
        in_specs=[scalars, scalars, blocks, blocks, blocks],
        out_specs=blocks,
    )(chan, kernel_weights, averaged, low, high)


def local(visibilities, model, flags, gains, kernel_weights):
    channels = visibilities.shape[0]
    place = jnp.stack([lax.axis_index("row"), lax.axis_index("col")]).astype(jnp.int32)
    first = lax.axis_index("chan") * channels
    total_channels = channels * lax.axis_size("chan")
    for step in range(ITERS):
        sums = sweep(step == 0, step == ITERS - 1, False, place, model, visibilities, flags, gains)
        parts = lax.all_to_all(sums, GRID, 0, 0)
        parts = parts.reshape(4, 4, *parts.shape[1:])
        total = parts[:, :, 0].sum(1) + parts[:, :, 1].sum(0)
        averaged = 0.5 * total[:, :2] / (total[:, 2:] + 1.0)
        mine = smooth(step == ITERS - 1, averaged, kernel_weights, first, total_channels)
        gains = lax.all_to_all(mine, GRID, 0, 0)
    residual, gains_out = finish(place, model, visibilities, flags, gains)
    return gains_out, residual


def solution(mesh):
    placed = (
        P("chan", None, None, None, "row", "col"),
        P(None, "chan", None, None, None, "row", "col"),
        P("chan", "row", "col"),
        P(None, None, None, "chan", None),
        P(),
    )
    return jax.shard_map(
        local,
        mesh=mesh,
        in_specs=placed,
        out_specs=(P(None, None, None, "chan", None), P("chan", None, None, None, "row", "col")),
        check_vma=False,
    )
```

```python
import functools

import jax
import jax.numpy as jnp
import numpy as np
from jax import lax
from jax.experimental import pallas as pl
from jax.experimental.pallas import tpu as pltpu
from jax.sharding import PartitionSpec as P

ITERS = 3
GRID = ("row", "col")
VMEM_LIMIT = 60 * 1024 * 1024
TILE = 16


def spread_matrix(count):
    spread = np.zeros((count, 2, 2, count, 2, TILE), np.float32)
    for k in range(count):
        spread[k, 0, 0, k, 0] = 1.0
        spread[k, 1, 0, k, 1] = -1.0
        spread[k, 1, 1, k, 0] = 1.0
        spread[k, 0, 1, k, 1] = 1.0
    return spread.reshape(2 * count, 4 * count * TILE)


def split(value):
    high = value.astype(jnp.bfloat16)
    low = (value - high.astype(jnp.float32)).astype(jnp.bfloat16)
    return high, low


def kernel(first, precise, final, place, *refs):
    refs = list(refs)
    take = refs.pop
    model, vis, flags, spread = take(0), take(0), take(0), take(0)
    if first:
        row_in, col_in = take(0), take(0)
    else:
        gains_in = take(0)
    if final:
        resid, gains_out = take(0), take(0)
    else:
        sums_out = take(0)
    g_row, g_col, g_mat, w_row, w_col, left, masked, raw = refs
    count = model.shape[0]
    channel = pl.program_id(0)
    me_row, me_col = place[0], place[1]
    f32, bf16 = jnp.float32, jnp.bfloat16

    @pl.when(channel == 0)
    def prepare():
        if first:
            g_row[...] = row_in[...]
            g_col[...] = col_in[...]
        else:
            for k in range(count):
                for pol in range(2):
                    for part in range(2):
                        if final:
                            g_row[k, part, pol] = gains_in[2 * k + pol, me_row, part]
                            g_col[k, part, pol] = gains_in[2 * k + pol, me_col, part]
                            for block in range(4):
                                lanes = slice(block * 128, block * 128 + 128)
                                gains_out[k, part, pol, :, lanes] = gains_in[2 * k + pol, block, part]
                        else:
                            g_row[k, part, pol] = gains_in[2 * k + pol, 0, part]
                            g_col[k, part, pol] = gains_in[2 * k + pol, 1, part]
        if not final:
            w_row[...] = jnp.zeros_like(w_row)
            w_col[...] = jnp.zeros_like(w_col)
        for k in range(count):
            for pol in range(2):
                lanes = slice(pol * 128, pol * 128 + 128)
                for part in range(2):
                    g_mat[:, 2 * k + part, lanes] = g_row[k, part, pol]
                if not final:
                    for source, weights in ((g_row, w_row), (g_col, w_col)):
                        re, im = source[k, 0, pol], source[k, 1, pol]
                        for n, value in enumerate((re, im, re * re + im * im)):
                            high = value.astype(bf16).astype(f32)
                            weights[:, k, n, lanes] = high
                            weights[:, k, 4 + n, lanes] = value - high

    gains_c = jnp.transpose(g_mat[channel])
    high, low = split(gains_c)
    width = 2 * count * TILE
    same = (
        lax.broadcasted_iota(jnp.int32, (128, 2 * width), 0) % TILE
        == lax.broadcasted_iota(jnp.int32, (128, 2 * width), 1) % TILE
    )
    for h, value in enumerate((high, low)):
        for pol in range(2):
            wide = jnp.dot(value[pol * 128 : pol * 128 + 128], spread[...], preferred_element_type=f32)
            wide = jnp.where(same, wide, 0.0).astype(bf16)
            for part in range(2):
                left[pol, :, (2 * h + part) * TILE : (2 * h + part + 1) * TILE, :] = wide[
                    :, part * width : (part + 1) * width
                ].reshape(128 // TILE, TILE, width)

    def residual_tile(step, _):
        pol, tile = step // 8, step % 8
        rows = pl.ds(pl.multiple_of(tile * TILE, TILE), TILE)
        stacks = []
        for b in range(2):
            parts, lows = [], []
            for k in range(count):
                m_re = model[k, 0, 0, 2 * pol + b, 0, rows, :].astype(f32)
                m_im = model[k, 0, 0, 2 * pol + b, 1, rows, :].astype(f32)
                q_re = g_col[k, 0, b, pl.ds(channel, 1), :]
                q_im = g_col[k, 1, b, pl.ds(channel, 1), :]
                z_re = m_re * q_re + m_im * q_im
                z_im = m_im * q_re - m_re * q_im
                for z in (z_re, z_im):
                    if final:
                        z_high, z_low = split(z)
                        parts.append(z_high)
                        lows.append(z_low)
                    else:
                        parts.append(z.astype(bf16))
            stacks.append((jnp.concatenate(parts, 0), jnp.concatenate(lows, 0) if final else None))
        gains_t = left[pol, tile]
        guess = jnp.dot(gains_t, jnp.concatenate([s[0] for s in stacks], 1), preferred_element_type=f32)
        if final:
            guess += jnp.dot(gains_t, jnp.concatenate([s[1] for s in stacks], 1), preferred_element_type=f32)
        weight = flags[0, rows, :].astype(f32)
        out_rows = pl.ds(pl.multiple_of(step * TILE, TILE), TILE)
        for b in range(2):
            for part in range(2):
                lanes = slice(b * 128, b * 128 + 128)
                total = (
                    guess[part * TILE : (part + 1) * TILE, lanes]
                    + guess[(2 + part) * TILE : (3 + part) * TILE, lanes]
                )
                seen = vis[0, 0, 2 * pol + b, part, rows, :].astype(f32)
                value = (seen - total) * weight
                if final:
                    resid[0, 0, 2 * pol + b, part, rows, :] = value.astype(bf16)
                else:
                    masked[part, out_rows, lanes] = value
        return 0

    if final:
        lax.fori_loop(0, 16, residual_tile, 0, unroll=4)
        return

    lax.fori_loop(0, 16, residual_tile, 0, unroll=4)
    weight = flags[0].astype(f32).astype(bf16)

    def sums(k, _):
        kinds = 5 if precise else 3
        planes = [[] for _ in range(kinds)]
        for pol in range(2):
            halves = [[] for _ in range(kinds)]
            for b in range(2):
                low_re = model[k, 0, 0, 2 * pol + b, 0]
                low_im = model[k, 0, 0, 2 * pol + b, 1]
                r_re = masked[0, pol * 128 : pol * 128 + 128, b * 128 : b * 128 + 128]
                r_im = masked[1, pol * 128 : pol * 128 + 128, b * 128 : b * 128 + 128]
                m_re, m_im = low_re.astype(f32), low_im.astype(f32)
                values = (r_re * m_re + r_im * m_im, r_im * m_re - r_re * m_im)
                values = split(values[0]) + split(values[1]) if precise else tuple(v.astype(bf16) for v in values)
                values += ((low_re * low_re + low_im * low_im) * weight,)
                for half, value in zip(halves, values):
                    half.append(value)
            for plane, half in zip(planes, halves):
                plane.append(jnp.concatenate(half, 1))
        planes = [jnp.concatenate(plane, 0) for plane in planes]
        by_q, by_p = w_col[channel, k].astype(bf16), w_row[channel, k].astype(bf16)
        over_q = [
            lax.dot_general(by_q, plane, (((1,), (1,)), ((), ())), preferred_element_type=f32) for plane in planes
        ]
        over_p = [jnp.dot(by_p, plane, preferred_element_type=f32) for plane in planes]
        for side, found in enumerate((over_q, over_p)):
            if precise:
                found = (found[0] + found[1], found[2] + found[3], found[4])
            for x, value in enumerate(found):
                raw[side, channel, k, x] = value[0:4] + value[4:8]
        return 0

    lax.fori_loop(0, count, sums, 0, unroll=8)
    last = pl.num_programs(0) - 1

    @pl.when(channel == last)
    def finish():
        for side, gains in ((0, g_row), (1, g_col)):
            sign = 1.0 if side == 0 else -1.0
            for k in range(count):
                for pol in range(2):
                    lanes = slice(pol * 128, pol * 128 + 128)
                    take_row = lambda x, n: raw[side, :, k, x, n, lanes]
                    denom = take_row(2, 2)
                    factor = 2.0 * denom + 0.25 if side == 0 else 2.0 * denom
                    top_re = take_row(0, 0) - sign * take_row(1, 1)
                    top_im = take_row(0, 1) + sign * take_row(1, 0)
                    sums_out[2 * k + pol, side, 0] = top_re + gains[k, 0, pol] * factor
                    sums_out[2 * k + pol, side, 1] = top_im + gains[k, 1, pol] * factor
                    sums_out[2 * k + pol, side, 2] = denom


def final_kernel(place, model, vis, flags, gains_in, resid, gains_out, p_rows, p_cols, q_rows):
    count = model.shape[0]
    channel = pl.program_id(0)
    me_row, me_col = place[0], place[1]
    f32, bf16 = jnp.float32, jnp.bfloat16

    @pl.when(channel == 0)
    def prepare():
        p_rows[...] = jnp.zeros_like(p_rows)
        for k in range(count):
            for pol in range(2):
                for part in range(2):
                    for block in range(4):
                        lanes = slice(block * 128, block * 128 + 128)
                        gains_out[k, part, pol, :, lanes] = gains_in[2 * k + pol, block, part]
                    p_rows[:, 2 * k + part, pol * 128 : pol * 128 + 128] = gains_in[2 * k + pol, me_row, part]
                re, im = gains_in[2 * k + pol, me_col, 0], gains_in[2 * k + pol, me_col, 1]
                for n, value in enumerate((im, re - im, re + im)):
                    q_rows[k, n, pol] = value

    p_cols[...] = jnp.transpose(p_rows[channel])

    def tile_work(step, _):
        pol, tile = step // 8, step % 8
        rows = pl.ds(pl.multiple_of(tile * TILE, TILE), TILE)
        p_tile = p_cols[pl.ds(pl.multiple_of(step * TILE, TILE), TILE), :]
        totals = [[0.0, 0.0] for _ in range(2)]
        for k in range(count):
            p_re, p_im = [jnp.broadcast_to(p_tile[:, 2 * k + n : 2 * k + n + 1], (TILE, 128)) for n in range(2)]
            for b in range(2):
                q = [q_rows[k, n, b, pl.ds(channel, 1), :] for n in range(3)]
                m_re = model[k, 0, 0, 2 * pol + b, 0, rows, :].astype(f32)
                m_im = model[k, 0, 0, 2 * pol + b, 1, rows, :].astype(f32)
                shared = q[0] * (m_re - m_im)
                z_re = m_re * q[2] - shared
                z_im = m_im * q[1] - shared
                totals[b][0] += p_re * z_re - p_im * z_im
                totals[b][1] += p_re * z_im + p_im * z_re
        weight = flags[0, rows, :].astype(f32)
        for b in range(2):
            for part in range(2):
                seen = vis[0, 0, 2 * pol + b, part, rows, :].astype(f32)
                resid[0, 0, 2 * pol + b, part, rows, :] = ((seen - totals[b][part]) * weight).astype(bf16)
        return 0

    lax.fori_loop(0, 16, tile_work, 0, unroll=4)


def finish(place, model, vis, flags, gains):
    count, channels = model.shape[0], model.shape[1]
    f32 = jnp.float32

    def whole(shape):
        return pl.BlockSpec(shape, lambda c, place: (0,) * len(shape))

    out_gains = (count, 2, 2, channels, 512)
    seen = pl.BlockSpec((1, 1, 4, 2, 128, 128), lambda c, place: (c, 0, 0, 0, 0, 0))
    return pl.pallas_call(
        final_kernel,
        out_shape=[jax.ShapeDtypeStruct(vis.shape, vis.dtype), jax.ShapeDtypeStruct(out_gains, f32)],
        grid_spec=pltpu.PrefetchScalarGridSpec(
            num_scalar_prefetch=1,
            grid=(channels,),
            in_specs=[
                pl.BlockSpec((count, 1, 1, 4, 2, 128, 128), lambda c, place: (0, c, 0, 0, 0, 0, 0)),
                seen,
                pl.BlockSpec((1, 128, 128), lambda c, place: (c, 0, 0)),
                whole(gains.shape),
            ],
            out_specs=[seen, whole(out_gains)],
            scratch_shapes=[
                pltpu.VMEM((channels, 128, 256), f32),
                pltpu.VMEM((256, 128), f32),
                pltpu.VMEM((count, 3, 2, channels, 128), f32),
            ],
        ),
        compiler_params=pltpu.CompilerParams(vmem_limit_bytes=VMEM_LIMIT),
        cost_estimate=pl.CostEstimate(flops=10**9, bytes_accessed=20 * 10**6, transcendentals=0),
    )(place, model, vis, flags, gains)


def sweep(first, precise, final, place, model, vis, flags, gains):
    count, channels = model.shape[0], model.shape[1]
    f32, bf16 = jnp.float32, jnp.bfloat16
    spread = jnp.asarray(spread_matrix(count), bf16)

    def whole(shape):
        return pl.BlockSpec(shape, lambda c, place: (0,) * len(shape))

    in_specs = [
        pl.BlockSpec((count, 1, 1, 4, 2, 128, 128), lambda c, place: (0, c, 0, 0, 0, 0, 0)),
        pl.BlockSpec((1, 1, 4, 2, 128, 128), lambda c, place: (c, 0, 0, 0, 0, 0)),
        pl.BlockSpec((1, 128, 128), lambda c, place: (c, 0, 0)),
        whole(spread.shape),
    ]
    if first:
        block = (count, 2, 2, channels, 128)
        in_specs += [
            pl.BlockSpec(block, lambda c, place: (0, 0, 0, 0, place[0])),
            pl.BlockSpec(block, lambda c, place: (0, 0, 0, 0, place[1])),
        ]
    else:
        in_specs += [whole(gains.shape)]
    if final:
        out_gains = (count, 2, 2, channels, 512)
        out_shape = [jax.ShapeDtypeStruct(vis.shape, bf16), jax.ShapeDtypeStruct(out_gains, f32)]
        out_specs = [pl.BlockSpec((1, 1, 4, 2, 128, 128), lambda c, place: (c, 0, 0, 0, 0, 0)), whole(out_gains)]
    else:
        shape = (2 * count, 2, 3, channels, 128)
        out_shape = jax.ShapeDtypeStruct(shape, f32)
        out_specs = whole(shape)
    return pl.pallas_call(
        functools.partial(kernel, first, precise, final),
        out_shape=out_shape,
        grid_spec=pltpu.PrefetchScalarGridSpec(
            num_scalar_prefetch=1,
            grid=(channels,),
            in_specs=in_specs,
            out_specs=out_specs,
            scratch_shapes=[
                pltpu.VMEM((count, 2, 2, channels, 128), f32),
                pltpu.VMEM((count, 2, 2, channels, 128), f32),
                pltpu.VMEM((channels, 2 * count, 256), f32),
                pltpu.VMEM((channels, count, 16, 256), f32),
                pltpu.VMEM((channels, count, 16, 256), f32),
                pltpu.VMEM((2, 8, 4 * TILE, 2 * count * TILE), bf16),
                pltpu.VMEM((2, 256, 256), f32),
                pltpu.VMEM((2, channels, count, 3, 4, 256), f32),
            ],
        ),
        compiler_params=pltpu.CompilerParams(vmem_limit_bytes=VMEM_LIMIT),
        cost_estimate=pl.CostEstimate(flops=10**10, bytes_accessed=20 * 10**6, transcendentals=0),
    )(place, model, vis, flags, spread, *((gains, gains) if first else (gains,)))


def smooth_kernel(everything, chan, weights, averaged, low, high, out):
    channels = averaged.shape[2]
    span = weights.shape[0]
    reach = span // 2
    index = chan[0] + lax.broadcasted_iota(jnp.int32, (channels, 128), 0)
    coverage = jnp.zeros((channels, 128), jnp.float32)
    for offset in range(span):
        source = index + (offset - reach)
        inside = ((source >= 0) & (source < chan[1])).astype(jnp.float32)
        coverage = coverage + weights[offset] * inside
    for block in range(4):
        for part in range(2):
            padded = jnp.concatenate([low[block, part], averaged[block, part], high[block, part]], 0)
            total = weights[0] * padded[0:channels]
            for offset in range(1, span):
                total = total + weights[offset] * padded[offset : offset + channels]
            value = total / coverage
            for target in range(16):
                if everything:
                    out[target, block, part] = value
                else:
                    if target // 4 == block:
                        out[target, 0, part] = value
                    if target % 4 == block:
                        out[target, 1, part] = value


def smooth(everything, averaged, kernel_weights, first, total_channels):
    reach = kernel_weights.shape[0] // 2
    channels = averaged.shape[2]
    chans = lax.axis_size("chan")
    low = lax.ppermute(averaged[:, :, channels - reach :], "chan", [(i, i + 1) for i in range(chans - 1)])
    high = lax.ppermute(averaged[:, :, :reach], "chan", [(i + 1, i) for i in range(chans - 1)])
    chan = jnp.stack([first, jnp.int32(total_channels)]).astype(jnp.int32)
    scalars = pl.BlockSpec(memory_space=pltpu.SMEM)
    blocks = pl.BlockSpec(memory_space=pltpu.VMEM)
    return pl.pallas_call(
        functools.partial(smooth_kernel, everything),
        out_shape=jax.ShapeDtypeStruct((16, 4 if everything else 2, *averaged.shape[1:]), jnp.float32),
        in_specs=[scalars, scalars, blocks, blocks, blocks],
        out_specs=blocks,
    )(chan, kernel_weights, averaged, low, high)


def local(visibilities, model, flags, gains, kernel_weights):
    channels = visibilities.shape[0]
    place = jnp.stack([lax.axis_index("row"), lax.axis_index("col")]).astype(jnp.int32)
    first = lax.axis_index("chan") * channels
    total_channels = channels * lax.axis_size("chan")
    for step in range(ITERS):
        sums = sweep(step == 0, step == ITERS - 1, False, place, model, visibilities, flags, gains)
        parts = lax.all_to_all(sums, GRID, 0, 0)
        parts = parts.reshape(4, 4, *parts.shape[1:])
        total = parts[:, :, 0].sum(1) + parts[:, :, 1].sum(0)
        averaged = 0.5 * total[:, :2] / (total[:, 2:] + 1.0)
        mine = smooth(step == ITERS - 1, averaged, kernel_weights, first, total_channels)
        gains = lax.all_to_all(mine, GRID, 0, 0)
    residual, gains_out = finish(place, model, visibilities, flags, gains)
    return gains_out, residual


def solution(mesh):
    placed = (
        P("chan", None, None, None, "row", "col"),
        P(None, "chan", None, None, None, "row", "col"),
        P("chan", "row", "col"),
        P(None, None, None, "chan", None),
        P(),
    )
    return jax.shard_map(
        local,
        mesh=mesh,
        in_specs=placed,
        out_specs=(P(None, None, None, "chan", None), P("chan", None, None, None, "row", "col")),
        check_vma=False,
    )
```

```python
import functools

import jax
import jax.numpy as jnp
import numpy as np
from jax import lax
from jax.experimental import pallas as pl
from jax.experimental.pallas import tpu as pltpu
from jax.sharding import PartitionSpec as P

ITERS = 3
GRID = ("row", "col")
VMEM_LIMIT = 60 * 1024 * 1024
TILE = 16


def spread_matrix(count):
    spread = np.zeros((count, 2, 2, count, 2, TILE), np.float32)
    for k in range(count):
        spread[k, 0, 0, k, 0] = 1.0
        spread[k, 1, 0, k, 1] = -1.0
        spread[k, 1, 1, k, 0] = 1.0
        spread[k, 0, 1, k, 1] = 1.0
    return spread.reshape(2 * count, 4 * count * TILE)


def split(value):
    high = value.astype(jnp.bfloat16)
    low = (value - high.astype(jnp.float32)).astype(jnp.bfloat16)
    return high, low


def kernel(first, precise, final, place, *refs):
    refs = list(refs)
    take = refs.pop
    model, vis, flags, spread = take(0), take(0), take(0), take(0)
    if first:
        row_in, col_in = take(0), take(0)
    else:
        gains_in = take(0)
    if final:
        resid, gains_out = take(0), take(0)
    else:
        sums_out = take(0)
    g_row, g_col, g_mat, w_row, w_col, left, masked, raw = refs
    count = model.shape[0]
    channel = pl.program_id(0)
    me_row, me_col = place[0], place[1]
    f32, bf16 = jnp.float32, jnp.bfloat16

    @pl.when(channel == 0)
    def prepare():
        if first:
            g_row[...] = row_in[...]
            g_col[...] = col_in[...]
        else:
            for k in range(count):
                for pol in range(2):
                    for part in range(2):
                        if final:
                            g_row[k, part, pol] = gains_in[2 * k + pol, me_row, part]
                            g_col[k, part, pol] = gains_in[2 * k + pol, me_col, part]
                            for block in range(4):
                                lanes = slice(block * 128, block * 128 + 128)
                                gains_out[k, part, pol, :, lanes] = gains_in[2 * k + pol, block, part]
                        else:
                            g_row[k, part, pol] = gains_in[2 * k + pol, 0, part]
                            g_col[k, part, pol] = gains_in[2 * k + pol, 1, part]
        if not final:
            w_row[...] = jnp.zeros_like(w_row)
            w_col[...] = jnp.zeros_like(w_col)
        for k in range(count):
            for pol in range(2):
                lanes = slice(pol * 128, pol * 128 + 128)
                for part in range(2):
                    g_mat[:, 2 * k + part, lanes] = g_row[k, part, pol]
                if not final:
                    for source, weights in ((g_row, w_row), (g_col, w_col)):
                        re, im = source[k, 0, pol], source[k, 1, pol]
                        for n, value in enumerate((re, im, re * re + im * im)):
                            high = value.astype(bf16).astype(f32)
                            weights[:, k, n, lanes] = high
                            weights[:, k, 4 + n, lanes] = value - high

    gains_c = jnp.transpose(g_mat[channel])
    high, low = split(gains_c)
    width = 2 * count * TILE
    same = (
        lax.broadcasted_iota(jnp.int32, (128, 2 * width), 0) % TILE
        == lax.broadcasted_iota(jnp.int32, (128, 2 * width), 1) % TILE
    )
    for h, value in enumerate((high, low)):
        for pol in range(2):
            wide = jnp.dot(value[pol * 128 : pol * 128 + 128], spread[...], preferred_element_type=f32)
            wide = jnp.where(same, wide, 0.0).astype(bf16)
            for part in range(2):
                left[pol, :, (2 * h + part) * TILE : (2 * h + part + 1) * TILE, :] = wide[
                    :, part * width : (part + 1) * width
                ].reshape(128 // TILE, TILE, width)

    def residual_tile(step, _):
        pol, tile = step // 8, step % 8
        rows = pl.ds(pl.multiple_of(tile * TILE, TILE), TILE)
        stacks = []
        for b in range(2):
            parts, lows = [], []
            for k in range(count):
                m_re = model[k, 0, 0, 2 * pol + b, 0, rows, :].astype(f32)
                m_im = model[k, 0, 0, 2 * pol + b, 1, rows, :].astype(f32)
                q_re = g_col[k, 0, b, pl.ds(channel, 1), :]
                q_im = g_col[k, 1, b, pl.ds(channel, 1), :]
                z_re = m_re * q_re + m_im * q_im
                z_im = m_im * q_re - m_re * q_im
                for z in (z_re, z_im):
                    if final:
                        z_high, z_low = split(z)
                        parts.append(z_high)
                        lows.append(z_low)
                    else:
                        parts.append(z.astype(bf16))
            stacks.append((jnp.concatenate(parts, 0), jnp.concatenate(lows, 0) if final else None))
        gains_t = left[pol, tile]
        guess = jnp.dot(gains_t, jnp.concatenate([s[0] for s in stacks], 1), preferred_element_type=f32)
        if final:
            guess += jnp.dot(gains_t, jnp.concatenate([s[1] for s in stacks], 1), preferred_element_type=f32)
        weight = flags[0, rows, :].astype(f32)
        out_rows = pl.ds(pl.multiple_of(step * TILE, TILE), TILE)
        for b in range(2):
            for part in range(2):
                lanes = slice(b * 128, b * 128 + 128)
                total = (
                    guess[part * TILE : (part + 1) * TILE, lanes]
                    + guess[(2 + part) * TILE : (3 + part) * TILE, lanes]
                )
                seen = vis[0, 0, 2 * pol + b, part, rows, :].astype(f32)
                value = (seen - total) * weight
                if final:
                    resid[0, 0, 2 * pol + b, part, rows, :] = value.astype(bf16)
                else:
                    masked[part, out_rows, lanes] = value
        return 0

    if final:
        lax.fori_loop(0, 16, residual_tile, 0, unroll=4)
        return

    lax.fori_loop(0, 16, residual_tile, 0, unroll=8)
    weight = flags[0].astype(f32).astype(bf16)

    def sums(k, _):
        kinds = 5 if precise else 3
        planes = [[] for _ in range(kinds)]
        for pol in range(2):
            halves = [[] for _ in range(kinds)]
            for b in range(2):
                low_re = model[k, 0, 0, 2 * pol + b, 0]
                low_im = model[k, 0, 0, 2 * pol + b, 1]
                r_re = masked[0, pol * 128 : pol * 128 + 128, b * 128 : b * 128 + 128]
                r_im = masked[1, pol * 128 : pol * 128 + 128, b * 128 : b * 128 + 128]
                m_re, m_im = low_re.astype(f32), low_im.astype(f32)
                values = (r_re * m_re + r_im * m_im, r_im * m_re - r_re * m_im)
                values = split(values[0]) + split(values[1]) if precise else tuple(v.astype(bf16) for v in values)
                values += ((low_re * low_re + low_im * low_im) * weight,)
                for half, value in zip(halves, values):
                    half.append(value)
            for plane, half in zip(planes, halves):
                plane.append(jnp.concatenate(half, 1))
        planes = [jnp.concatenate(plane, 0) for plane in planes]
        by_q, by_p = w_col[channel, k].astype(bf16), w_row[channel, k].astype(bf16)
        over_q = [
            lax.dot_general(by_q, plane, (((1,), (1,)), ((), ())), preferred_element_type=f32) for plane in planes
        ]
        over_p = [jnp.dot(by_p, plane, preferred_element_type=f32) for plane in planes]
        for side, found in enumerate((over_q, over_p)):
            if precise:
                found = (found[0] + found[1], found[2] + found[3], found[4])
            for x, value in enumerate(found):
                raw[side, channel, k, x] = value[0:4] + value[4:8]
        return 0

    lax.fori_loop(0, count, sums, 0, unroll=8)
    last = pl.num_programs(0) - 1

    @pl.when(channel == last)
    def finish():
        for side, gains in ((0, g_row), (1, g_col)):
            sign = 1.0 if side == 0 else -1.0
            for k in range(count):
                for pol in range(2):
                    lanes = slice(pol * 128, pol * 128 + 128)
                    take_row = lambda x, n: raw[side, :, k, x, n, lanes]
                    denom = take_row(2, 2)
                    factor = 2.0 * denom + 0.25 if side == 0 else 2.0 * denom
                    top_re = take_row(0, 0) - sign * take_row(1, 1)
                    top_im = take_row(0, 1) + sign * take_row(1, 0)
                    sums_out[2 * k + pol, side, 0] = top_re + gains[k, 0, pol] * factor
                    sums_out[2 * k + pol, side, 1] = top_im + gains[k, 1, pol] * factor
                    sums_out[2 * k + pol, side, 2] = denom


def final_kernel(place, model, vis, flags, gains_in, resid, gains_out, p_rows, p_cols, q_rows):
    count = model.shape[0]
    channel = pl.program_id(0)
    me_row, me_col = place[0], place[1]
    f32, bf16 = jnp.float32, jnp.bfloat16

    @pl.when(channel == 0)
    def prepare():
        p_rows[...] = jnp.zeros_like(p_rows)
        for k in range(count):
            for pol in range(2):
                for part in range(2):
                    for block in range(4):
                        lanes = slice(block * 128, block * 128 + 128)
                        gains_out[k, part, pol, :, lanes] = gains_in[2 * k + pol, block, part]
                    p_rows[:, 2 * k + part, pol * 128 : pol * 128 + 128] = gains_in[2 * k + pol, me_row, part]
                re, im = gains_in[2 * k + pol, me_col, 0], gains_in[2 * k + pol, me_col, 1]
                for n, value in enumerate((im, re - im, re + im)):
                    q_rows[k, n, pol] = value

    p_cols[...] = jnp.transpose(p_rows[channel])

    def tile_work(step, _):
        pol, tile = step // 8, step % 8
        rows = pl.ds(pl.multiple_of(tile * TILE, TILE), TILE)
        p_tile = p_cols[pl.ds(pl.multiple_of(step * TILE, TILE), TILE), :]
        totals = [[0.0, 0.0] for _ in range(2)]
        for k in range(count):
            p_re, p_im = [jnp.broadcast_to(p_tile[:, 2 * k + n : 2 * k + n + 1], (TILE, 128)) for n in range(2)]
            for b in range(2):
                q = [q_rows[k, n, b, pl.ds(channel, 1), :] for n in range(3)]
                m_re = model[k, 0, 0, 2 * pol + b, 0, rows, :].astype(f32)
                m_im = model[k, 0, 0, 2 * pol + b, 1, rows, :].astype(f32)
                shared = q[0] * (m_re - m_im)
                z_re = m_re * q[2] - shared
                z_im = m_im * q[1] - shared
                totals[b][0] += p_re * z_re - p_im * z_im
                totals[b][1] += p_re * z_im + p_im * z_re
        weight = flags[0, rows, :].astype(f32)
        for b in range(2):
            for part in range(2):
                seen = vis[0, 0, 2 * pol + b, part, rows, :].astype(f32)
                resid[0, 0, 2 * pol + b, part, rows, :] = ((seen - totals[b][part]) * weight).astype(bf16)
        return 0

    lax.fori_loop(0, 16, tile_work, 0, unroll=4)


def finish(place, model, vis, flags, gains):
    count, channels = model.shape[0], model.shape[1]
    f32 = jnp.float32

    def whole(shape):
        return pl.BlockSpec(shape, lambda c, place: (0,) * len(shape))

    out_gains = (count, 2, 2, channels, 512)
    seen = pl.BlockSpec((1, 1, 4, 2, 128, 128), lambda c, place: (c, 0, 0, 0, 0, 0))
    return pl.pallas_call(
        final_kernel,
        out_shape=[jax.ShapeDtypeStruct(vis.shape, vis.dtype), jax.ShapeDtypeStruct(out_gains, f32)],
        grid_spec=pltpu.PrefetchScalarGridSpec(
            num_scalar_prefetch=1,
            grid=(channels,),
            in_specs=[
                pl.BlockSpec((count, 1, 1, 4, 2, 128, 128), lambda c, place: (0, c, 0, 0, 0, 0, 0)),
                seen,
                pl.BlockSpec((1, 128, 128), lambda c, place: (c, 0, 0)),
                whole(gains.shape),
            ],
            out_specs=[seen, whole(out_gains)],
            scratch_shapes=[
                pltpu.VMEM((channels, 128, 256), f32),
                pltpu.VMEM((256, 128), f32),
                pltpu.VMEM((count, 3, 2, channels, 128), f32),
            ],
        ),
        compiler_params=pltpu.CompilerParams(vmem_limit_bytes=VMEM_LIMIT),
        cost_estimate=pl.CostEstimate(flops=10**9, bytes_accessed=20 * 10**6, transcendentals=0),
    )(place, model, vis, flags, gains)


def sweep(first, precise, final, place, model, vis, flags, gains):
    count, channels = model.shape[0], model.shape[1]
    f32, bf16 = jnp.float32, jnp.bfloat16
    spread = jnp.asarray(spread_matrix(count), bf16)

    def whole(shape):
        return pl.BlockSpec(shape, lambda c, place: (0,) * len(shape))

    in_specs = [
        pl.BlockSpec((count, 1, 1, 4, 2, 128, 128), lambda c, place: (0, c, 0, 0, 0, 0, 0)),
        pl.BlockSpec((1, 1, 4, 2, 128, 128), lambda c, place: (c, 0, 0, 0, 0, 0)),
        pl.BlockSpec((1, 128, 128), lambda c, place: (c, 0, 0)),
        whole(spread.shape),
    ]
    if first:
        block = (count, 2, 2, channels, 128)
        in_specs += [
            pl.BlockSpec(block, lambda c, place: (0, 0, 0, 0, place[0])),
            pl.BlockSpec(block, lambda c, place: (0, 0, 0, 0, place[1])),
        ]
    else:
        in_specs += [whole(gains.shape)]
    if final:
        out_gains = (count, 2, 2, channels, 512)
        out_shape = [jax.ShapeDtypeStruct(vis.shape, bf16), jax.ShapeDtypeStruct(out_gains, f32)]
        out_specs = [pl.BlockSpec((1, 1, 4, 2, 128, 128), lambda c, place: (c, 0, 0, 0, 0, 0)), whole(out_gains)]
    else:
        shape = (2 * count, 2, 3, channels, 128)
        out_shape = jax.ShapeDtypeStruct(shape, f32)
        out_specs = whole(shape)
    return pl.pallas_call(
        functools.partial(kernel, first, precise, final),
        out_shape=out_shape,
        grid_spec=pltpu.PrefetchScalarGridSpec(
            num_scalar_prefetch=1,
            grid=(channels,),
            in_specs=in_specs,
            out_specs=out_specs,
            scratch_shapes=[
                pltpu.VMEM((count, 2, 2, channels, 128), f32),
                pltpu.VMEM((count, 2, 2, channels, 128), f32),
                pltpu.VMEM((channels, 2 * count, 256), f32),
                pltpu.VMEM((channels, count, 16, 256), f32),
                pltpu.VMEM((channels, count, 16, 256), f32),
                pltpu.VMEM((2, 8, 4 * TILE, 2 * count * TILE), bf16),
                pltpu.VMEM((2, 256, 256), f32),
                pltpu.VMEM((2, channels, count, 3, 4, 256), f32),
            ],
        ),
        compiler_params=pltpu.CompilerParams(vmem_limit_bytes=VMEM_LIMIT),
        cost_estimate=pl.CostEstimate(flops=10**10, bytes_accessed=20 * 10**6, transcendentals=0),
    )(place, model, vis, flags, spread, *((gains, gains) if first else (gains,)))


def smooth_kernel(everything, chan, weights, averaged, low, high, out):
    channels = averaged.shape[2]
    span = weights.shape[0]
    reach = span // 2
    index = chan[0] + lax.broadcasted_iota(jnp.int32, (channels, 128), 0)
    coverage = jnp.zeros((channels, 128), jnp.float32)
    for offset in range(span):
        source = index + (offset - reach)
        inside = ((source >= 0) & (source < chan[1])).astype(jnp.float32)
        coverage = coverage + weights[offset] * inside
    for block in range(4):
        for part in range(2):
            padded = jnp.concatenate([low[block, part], averaged[block, part], high[block, part]], 0)
            total = weights[0] * padded[0:channels]
            for offset in range(1, span):
                total = total + weights[offset] * padded[offset : offset + channels]
            value = total / coverage
            for target in range(16):
                if everything:
                    out[target, block, part] = value
                else:
                    if target // 4 == block:
                        out[target, 0, part] = value
                    if target % 4 == block:
                        out[target, 1, part] = value


def smooth(everything, averaged, kernel_weights, first, total_channels):
    reach = kernel_weights.shape[0] // 2
    channels = averaged.shape[2]
    chans = lax.axis_size("chan")
    low = lax.ppermute(averaged[:, :, channels - reach :], "chan", [(i, i + 1) for i in range(chans - 1)])
    high = lax.ppermute(averaged[:, :, :reach], "chan", [(i + 1, i) for i in range(chans - 1)])
    chan = jnp.stack([first, jnp.int32(total_channels)]).astype(jnp.int32)
    scalars = pl.BlockSpec(memory_space=pltpu.SMEM)
    blocks = pl.BlockSpec(memory_space=pltpu.VMEM)
    return pl.pallas_call(
        functools.partial(smooth_kernel, everything),
        out_shape=jax.ShapeDtypeStruct((16, 4 if everything else 2, *averaged.shape[1:]), jnp.float32),
        in_specs=[scalars, scalars, blocks, blocks, blocks],
        out_specs=blocks,
    )(chan, kernel_weights, averaged, low, high)


def local(visibilities, model, flags, gains, kernel_weights):
    channels = visibilities.shape[0]
    place = jnp.stack([lax.axis_index("row"), lax.axis_index("col")]).astype(jnp.int32)
    first = lax.axis_index("chan") * channels
    total_channels = channels * lax.axis_size("chan")
    for step in range(ITERS):
        sums = sweep(step == 0, step == ITERS - 1, False, place, model, visibilities, flags, gains)
        parts = lax.all_to_all(sums, GRID, 0, 0)
        parts = parts.reshape(4, 4, *parts.shape[1:])
        total = parts[:, :, 0].sum(1) + parts[:, :, 1].sum(0)
        averaged = 0.5 * total[:, :2] / (total[:, 2:] + 1.0)
        mine = smooth(step == ITERS - 1, averaged, kernel_weights, first, total_channels)
        gains = lax.all_to_all(mine, GRID, 0, 0)
    residual, gains_out = finish(place, model, visibilities, flags, gains)
    return gains_out, residual


def solution(mesh):
    placed = (
        P("chan", None, None, None, "row", "col"),
        P(None, "chan", None, None, None, "row", "col"),
        P("chan", "row", "col"),
        P(None, None, None, "chan", None),
        P(),
    )
    return jax.shard_map(
        local,
        mesh=mesh,
        in_specs=placed,
        out_specs=(P(None, None, None, "chan", None), P("chan", None, None, None, "row", "col")),
        check_vma=False,
    )
```
